512 devices in a mesh: expert: 128 (over z, y, core), replica: 4 (over x).
Axes of the slice: x: 4, y: 8, z: 8, core: 2. Of those that a mesh axis runs over, the one named last changes fastest.
Arguments:
- tokens: bfloat16 [16384, 6144], P('expert', 'replica'), may hold values from -6 to 6
- probe: bfloat16 [16384, 6144], P('expert', 'replica'), may hold values from -6 to 6
- cotangent: bfloat16 [16384, 1024], P('expert'), may hold values from -6 to 6
- expert_ids: int32 [16384, 1], P('expert'), may hold values from 0 to 127; in each aligned block of 128 rows (0 to 127, 128 to 255, ...) at most 2 rows name the same one
- weight: bfloat16 [128, 6144, 1024], P('expert', 'replica'), may hold values from -0.078125 to 0.078125
Outputs:
- grad_rows: bfloat16 [16384, 6144], P('expert', 'replica')
- hv_rows: bfloat16 [16384, 6144], P('expert', 'replica')
The draws below stay inside these ranges and needn't reach their ends.
Inputs may be any that keep to these rules, and one draw needn't show every extreme that they name: `expert_ids`: among the 128 tokens of one index of the expert axis at most 2 name the same expert; in every draw some index has exactly 2 tokens that name one expert.
All inputs are finite; a program needn't handle non-finite values.
Results may differ from the reference program's by a relative error of at most 0.0049.
Values may be sent and summed in bfloat16 or wider, within the bound.
A program may use at most 64 MiB of HBM per device.

```python
import math
import jax
import jax.numpy as jnp
import numpy as np
from jax import lax

D = 6144
FF = 1024
TOK_DEV = 128
EXPERTS = 128
CAP = 2
TOKENS = 16384
N_EXPERT = 128


def block_levels(key, shape, split, least, largest):
    level = 1.0
    for dim, blocks in split:
        heights = jax.random.uniform(jax.random.fold_in(jax.random.fold_in(key, 6), dim), (blocks,), jnp.float32, least / len(split), largest / len(split))
        level = level * jnp.repeat(jnp.exp(heights), shape[dim] // blocks).reshape((-1,) + (1,) * (len(shape) - 1 - dim))
    return level


def routed_block(stream_key, own, number, rows, number_of, top, limit, skew):
    order = jax.random.permutation(stream_key, number_of)
    packed, common = load_shares(number_of, rows * top, limit, skew, True), load_shares(number_of, rows * top, limit, skew, False)
    places = jnp.arange(number_of)

    def named(sizes, rotation):
        used = int((sizes > 0).sum())
        fixed = max(1, used // 4)
        moved = fixed + (places - fixed + rotation * (used - fixed)) % max(1, number_of - fixed)
        return jnp.zeros((number_of,), jnp.int32).at[order[jnp.where(places < fixed, places, moved)]].set(jnp.asarray(sizes, jnp.int32))

    sizes = jnp.where(number % 4 == 0, named(packed, number // 4), named(common, number - number // 4 - 1))
    mixed = jax.random.permutation(jax.random.fold_in(own, 3), number_of)
    giver, receiver = mixed[0:number_of // 2 * 2:2], mixed[1:number_of // 2 * 2:2]
    slack = jnp.minimum(sizes[giver] - 1, limit - sizes[receiver]) // 2
    slack = jnp.where((giver == order[0]) | (receiver == order[0]) | (sizes[receiver] == 0), 0, jnp.maximum(slack, 0))
    moved = jax.random.randint(jax.random.fold_in(own, 4), (number_of // 2,), 0, 1 << 20) % (slack + 1)
    sizes = sizes.at[giver].add(-moved).at[receiver].add(moved)
    members = jnp.searchsorted(jnp.cumsum(sizes), jnp.arange(rows * top), side="right").astype(jnp.int32)
    grid = members.reshape(top, rows).T
    grid = grid[jax.random.permutation(jax.random.fold_in(own, 1), rows)]
    rotation = jax.random.randint(jax.random.fold_in(own, 2), (rows, 1), 0, top)
    return jnp.take_along_axis(grid, (jnp.arange(top)[None, :] + rotation) % top, axis=1)


def load_shares(amount, total, limit, lean, full):
    loads = [(1 << 20) // math.isqrt(standing ** lean) + 1 for standing in range(1, amount + 1)]
    largest = limit if full else min(limit, max(-(-total // amount), total * loads[0] // sum(loads)))
    least = 1 if total - largest >= amount - 1 else 0
    given, spare = [largest] + [least] * (amount - 1), total - largest - least * (amount - 1)
    while spare > 0:
        free = [i for i in range(1, amount) if given[i] < largest] or [i for i in range(1, amount) if given[i] < limit]
        whole, remaining = sum([loads[i] for i in free]), spare
        for i in free:
            more = min(limit - given[i], max(1, remaining * loads[i] // whole), spare)
            given[i] = given[i] + more
            spare = spare - more
    return np.array(given)


def gaussian(key, shape, spread, limit, shards=(), kind=jnp.bfloat16):
    loudness = block_levels(key, shape, shards, -0.22, 0.18) if shards else 1.0
    values = jax.random.normal(key, shape, jnp.float32) * spread * loudness
    return jnp.minimum(jnp.maximum(values, -limit), limit).astype(kind)


def setup_inputs(seed: int = 0) -> dict:
    streams_of = jax.random.split(jax.random.key(seed), 6)
    tokens = gaussian(streams_of[0], (TOKENS, D), 1.0, 6.0, ((0, 128), (1, 4)))
    probe = gaussian(streams_of[1], (TOKENS, D), 1.0, 6.0, ((0, 128), (1, 4)))
    cotangent = gaussian(streams_of[2], (TOKENS, FF), 1.0, 6.0, ((0, 128),))
    expert_ids_keys = jax.random.split(jax.random.fold_in(streams_of[3], 1), TOKENS // TOK_DEV)
    expert_ids_turns = jax.random.permutation(jax.random.fold_in(streams_of[3], 3), TOKENS // TOK_DEV)
    expert_ids = jax.vmap(lambda own, number: routed_block(jax.random.fold_in(streams_of[3], 2), own, number, TOK_DEV, EXPERTS, 1, CAP, 2))(expert_ids_keys, expert_ids_turns).reshape((TOKENS, 1))
    weight = gaussian(streams_of[4], (EXPERTS, D, FF), D ** -0.5, 0.078125, ((0, 128), (1, 4)))
    return dict(tokens=tokens, probe=probe, cotangent=cotangent, expert_ids=expert_ids, weight=weight)


def derivatives(pre):
    sig = jax.nn.sigmoid(pre)
    first = sig * (1.0 + pre * (1.0 - sig))
    second = sig * (1.0 - sig) * (2.0 + pre * (1.0 - 2.0 * sig))
    return first, second


def reference(tokens, probe, cotangent, expert_ids, weight):
    ids = expert_ids[:, 0].astype(jnp.int32)
    total = ids.shape[0]
    order = jnp.argsort(ids, stable=True).astype(jnp.int32)
    sorted_ids = ids[order]
    counts = jnp.sum((ids[:, None] == jnp.arange(EXPERTS, dtype=jnp.int32)[None, :]).astype(jnp.int32), axis=0)
    starts = (jnp.cumsum(counts) - counts).astype(jnp.int32)
    rank_sorted = jnp.arange(total, dtype=jnp.int32) - starts[sorted_ids]
    rank = jnp.zeros((total,), jnp.int32).at[order].set(rank_sorted)
    most = N_EXPERT * CAP
    table = jnp.full((EXPERTS, most), total, jnp.int32).at[ids, rank].set(jnp.arange(total, dtype=jnp.int32))
    width = tokens.shape[1]
    tokens_pad = jnp.concatenate([tokens, jnp.zeros((1, width), tokens.dtype)], axis=0)
    probe_pad = jnp.concatenate([probe, jnp.zeros((1, width), probe.dtype)], axis=0)
    cot_pad = jnp.concatenate([cotangent, jnp.zeros((1, cotangent.shape[1]), cotangent.dtype)], axis=0)

    def one_expert(index, carry):
        grads, hvs = carry
        rows = table[index]
        mat = weight[index]
        pre = jnp.dot(tokens_pad[rows], mat, preferred_element_type=jnp.float32)
        pre_dot = jnp.dot(probe_pad[rows], mat, preferred_element_type=jnp.float32)
        cot = cot_pad[rows].astype(jnp.float32)
        first_d, second_d = derivatives(pre)
        first = (cot * first_d).astype(jnp.bfloat16)
        second = (cot * second_d * pre_dot).astype(jnp.bfloat16)
        dims = (((1,), (1,)), ((), ()))
        grad_part = lax.dot_general(first, mat, dims, preferred_element_type=jnp.float32).astype(jnp.bfloat16)
        hv_part = lax.dot_general(second, mat, dims, preferred_element_type=jnp.float32).astype(jnp.bfloat16)
        grads = grads.at[rows].set(grad_part, mode="drop")
        hvs = hvs.at[rows].set(hv_part, mode="drop")
        return grads, hvs

    start = (jnp.zeros((total, width), jnp.bfloat16), jnp.zeros((total, width), jnp.bfloat16))
    grad_rows, hv_rows = lax.fori_loop(0, EXPERTS, one_expert, start)
    return grad_rows, hv_rows
```

```python
import functools

import jax
import jax.numpy as jnp
from jax import lax
from jax.experimental import pallas as pl
from jax.experimental.pallas import tpu as pltpu
from jax.sharding import PartitionSpec as P

MESH = pl.DeviceIdType.MESH
F32 = jnp.float32
BF16 = jnp.bfloat16


def mm(a, b):
    return jnp.dot(a, b, preferred_element_type=F32)


def iota(shape, dim):
    return lax.broadcasted_iota(jnp.int32, shape, dim)


def transpose_matrix(a, b):
    row, col = iota((a * b, a * b), 0), iota((a * b, a * b), 1)
    return jnp.where((row % b) * a + row // b == col, 1.0, 0.0).astype(BF16)


def kernel(
    zs, ys, reps,
    x_ref, p_ref, cot_ref, ids_ref, w_hbm,
    grad_ref, hv_ref,
    w, fsend, frecv, csend, crecv, part, rsrecv, act, bsend, brecv, rows,
    to_blocks, from_blocks, cot_to, cot_from,
    w_sem, f_ss, f_rs, c_ss, c_rs, r_ss, r_rs, a_ss, a_rs, b_ss, b_rs,
):
    experts = 2 * zs * ys
    m = 2 * zs
    n, width = x_ref.shape
    kc = width // 4
    ffq = part.shape[2] // reps
    me = lax.axis_index("expert")
    rep = lax.axis_index("replica")
    core = lax.rem(me, 2)
    y = lax.rem(me // 2, ys)
    z = me // (2 * ys)

    def dest(c, i):
        dz, rc = i // 2, lax.rem(i, 2)
        zz, yy = lax.rem(z + dz, zs), lax.rem(y + dz + c, ys)
        return (zz * ys + yy) * 2 + lax.rem(core + rc, 2)

    def source(c, i):
        dz, rc = i // 2, lax.rem(i, 2)
        zz, yy = lax.rem(z + zs - dz, zs), lax.rem(y + (zs + 2) * ys - dz - c, ys)
        return (zz * ys + yy) * 2 + lax.rem(core + rc, 2)

    w_copy = pltpu.make_async_copy(w_hbm, w, w_sem)
    w_copy.start()

    barrier = pltpu.get_barrier_semaphore()

    def greet(i, carry):
        pl.semaphore_signal(
            barrier, inc=1, device_id=(lax.rem(me + i, experts), rep), device_id_type=MESH
        )
        return carry

    for j in range(1, reps):
        pl.semaphore_signal(
            barrier, inc=1, device_id=(me, lax.rem(rep + j, reps)), device_id_type=MESH
        )
    lax.fori_loop(1, experts, greet, 0)

    ids_col = ids_ref[...]
    row, col = iota((n, n), 0), iota((n, n), 1)
    ids_row = jnp.sum(
        jnp.where(row == col, ids_col.astype(F32), 0.0), axis=0, keepdims=True
    ).astype(jnp.int32)
    same = ids_col == ids_row
    slot_row = jnp.sum(
        jnp.where(same & (row < col), 1.0, 0.0), axis=0, keepdims=True
    ).astype(jnp.int32)
    slot_col = jnp.sum(
        jnp.where(same & (col < row), 1.0, 0.0), axis=1, keepdims=True
    ).astype(jnp.int32)

    def target(ids, slot):
        to_core, to_y, to_z = ids % 2, (ids // 2) % ys, ids // (2 * ys)
        dz = (to_z - z + zs) % zs
        c = (to_y - y - dz + (zs + 2) * ys) % ys
        return c * (2 * m) + slot * m + dz * 2 + (to_core + core) % 2

    tgt_row = target(ids_row, slot_row)
    tgt_col = target(ids_col, slot_col)

    to_blocks[...] = transpose_matrix(m, 16)
    from_blocks[...] = transpose_matrix(16, m)
    cot_to[...] = transpose_matrix(m, 4)
    cot_from[...] = transpose_matrix(4, m)

    def whole(ref, c, sem, own):
        if not own:
            pltpu.make_async_copy(ref.at[c], ref.at[c], sem.at[c]).wait()
            return

        @pl.when(c == 0)
        def _():
            some = ref.at[0, pl.ds(1, m - 1)]
            pltpu.make_async_copy(some, some, sem.at[0]).wait()

        @pl.when(c > 0)
        def _():
            pltpu.make_async_copy(ref.at[c], ref.at[c], sem.at[c]).wait()

    def blocks(stacked):
        tall = jnp.concatenate([stacked[:, k * kc:(k + 1) * kc] for k in range(4)], axis=0)
        return mm(to_blocks[...], tall).astype(BF16).reshape(m, 16, kc)

    def unblock(block):
        tall = mm(from_blocks[...], block.reshape(m * 16, kc)).astype(BF16)
        return jnp.concatenate([tall[k * 4 * m:(k + 1) * 4 * m] for k in range(4)], axis=1)

    def pack(c):
        route = jnp.where(iota((2 * m, n), 0) + c * (2 * m) == tgt_row, 1.0, 0.0).astype(BF16)
        xs = mm(route, x_ref[...]).astype(BF16)
        ps = mm(route, p_ref[...]).astype(BF16)
        block = blocks(jnp.concatenate([xs, ps], axis=0))
        fsend[c] = block
        mine = cot_ref[:, pl.ds(pl.multiple_of(rep * ffq, ffq), ffq)]
        cs = mm(route, mine).astype(BF16)
        half = ffq // 2
        tall = jnp.concatenate([cs[:, :half], cs[:, half:]], axis=0)
        cblock = mm(cot_to[...], tall).astype(BF16).reshape(m, 4, half)
        csend[c] = cblock

        @pl.when(c == 0)
        def _():
            frecv[0, 0] = block[0]
            crecv[0, 0] = cblock[0]

    def send(c, first):
        def one(i, carry):
            to = (dest(c, i), rep)
            pltpu.make_async_remote_copy(
                src_ref=fsend.at[c, i], dst_ref=frecv.at[c, i],
                send_sem=f_ss.at[c], recv_sem=f_rs.at[c],
                device_id=to, device_id_type=MESH,
            ).start()
            pltpu.make_async_remote_copy(
                src_ref=csend.at[c, i], dst_ref=crecv.at[c, i],
                send_sem=c_ss.at[c], recv_sem=c_rs.at[c],
                device_id=to, device_id_type=MESH,
            ).start()
            return carry

        lax.fori_loop(first, m, one, 0)

    pack(0)
    pl.semaphore_wait(barrier, experts - 1 + reps - 1)
    send(0, 1)

    def dispatch(c, carry):
        pack(c)
        send(c, 0)
        return carry

    lax.fori_loop(1, ys, dispatch, 0)
    w_copy.wait()

    def quarter(r):
        return pl.ds(pl.multiple_of(r * ffq, ffq), ffq)

    def project(c):
        whole(frecv, c, f_rs, True)
        part[c] = mm(unblock(frecv[c]), w[...])
        for j in range(1, reps):
            to = lax.rem(rep + j, reps)
            pltpu.make_async_remote_copy(
                src_ref=part.at[c, :, quarter(to)], dst_ref=rsrecv.at[c, j - 1],
                send_sem=r_ss.at[c], recv_sem=r_rs.at[c],
                device_id=(me, to), device_id_type=MESH,
            ).start()

    def activate(c):
        whole(rsrecv, c, r_rs, False)
        whole(crecv, c, c_rs, True)
        total = part[c, :, quarter(rep)]
        for j in range(reps - 1):
            total = total + rsrecv[c, j]
        pre, pre_dot = total[:2 * m], total[2 * m:]
        half = ffq // 2
        tall = mm(cot_from[...], crecv[c].reshape(4 * m, half))
        cot = jnp.concatenate([tall[:2 * m], tall[2 * m:]], axis=1)
        sig = 1.0 / (1.0 + jnp.exp(-pre))
        first = cot * (sig * (1.0 + pre * (1.0 - sig)))
        second = cot * (sig * (1.0 - sig) * (2.0 + pre * (1.0 - 2.0 * sig))) * pre_dot
        act[c, :, quarter(rep)] = jnp.concatenate([first, second], axis=0).astype(BF16)
        for j in range(1, reps):
            to = lax.rem(rep + j, reps)
            pltpu.make_async_remote_copy(
                src_ref=act.at[c, :, quarter(rep)], dst_ref=act.at[c, :, quarter(rep)],
                send_sem=a_ss.at[c], recv_sem=a_rs.at[c],
                device_id=(me, to), device_id_type=MESH,
            ).start()

    def others(ref, c, sem):
        some = ref.at[c, :, pl.ds(0, (reps - 1) * ffq)]
        pltpu.make_async_copy(some, some, sem.at[c]).wait()

    def give_back(c):
        others(act, c, a_rs)
        back = lax.dot_general(
            act[c], w[...], (((1,), (1,)), ((), ())), preferred_element_type=F32
        ).astype(BF16)
        block = blocks(back)
        bsend[c] = block

        @pl.when(c == 0)
        def _():
            brecv[0, 0] = block[0]

        def one(i, carry):
            @pl.when(c + i > 0)
            def _():
                pltpu.make_async_remote_copy(
                    src_ref=bsend.at[c, i], dst_ref=brecv.at[c, i],
                    send_sem=b_ss.at[c], recv_sem=b_rs.at[c],
                    device_id=(source(c, i), rep), device_id_type=MESH,
                ).start()
            return carry

        lax.fori_loop(0, m, one, 0)

    def step(s, carry):
        @pl.when(s < ys)
        def _():
            project(s)

        @pl.when((s >= 1) & (s < ys + 1))
        def _():
            activate(s - 1)

        @pl.when(s >= 2)
        def _():
            give_back(s - 2)

        return carry

    lax.fori_loop(0, ys + 2, step, 0)

    def collect(c, carry):
        whole(brecv, c, b_rs, True)
        got = unblock(brecv[c])
        at = pl.ds(pl.multiple_of(c * 2 * m, 2 * m), 2 * m)
        rows[0, at, :] = got[:2 * m]
        rows[1, at, :] = got[2 * m:]
        return carry

    lax.fori_loop(0, ys, collect, 0)

    pick = jnp.where(iota((n, 2 * m * ys), 1) == tgt_col, 1.0, 0.0).astype(BF16)
    grad_ref[...] = mm(pick, rows[0]).astype(BF16)
    hv_ref[...] = mm(pick, rows[1]).astype(BF16)

    def drain(c, carry):
        whole(fsend, c, f_ss, True)
        whole(csend, c, c_ss, True)
        whole(bsend, c, b_ss, True)
        others(part, c, r_ss)
        others(act, c, a_ss)
        return carry

    lax.fori_loop(0, ys, drain, 0)


def solution(mesh):
    experts, reps = mesh.shape["expert"], mesh.shape["replica"]
    zs = {128: 8, 8: 2}[experts]
    ys = experts // (2 * zs)
    m = 2 * zs

    def shards(tokens, probe, cotangent, expert_ids, weight):
        n, width = tokens.shape
        ff = weight.shape[2]
        ffq = ff // reps
        kc = width // 4
        vmem = pl.BlockSpec(memory_space=pltpu.VMEM)
        dma = pltpu.SemaphoreType.DMA
        return pl.pallas_call(
            functools.partial(kernel, zs, ys, reps),
            out_shape=[jax.ShapeDtypeStruct((n, width), BF16)] * 2,
            in_specs=[vmem] * 4 + [pl.BlockSpec(memory_space=pl.ANY)],
            out_specs=[vmem] * 2,
            scratch_shapes=[
                pltpu.VMEM((width, ff), BF16),
                pltpu.VMEM((ys, m, 16, kc), BF16),
                pltpu.VMEM((ys, m, 16, kc), BF16),
                pltpu.VMEM((ys, m, 4, ffq // 2), BF16),
                pltpu.VMEM((ys, m, 4, ffq // 2), BF16),
                pltpu.VMEM((ys, 4 * m, ff), F32),
                pltpu.VMEM((ys, reps - 1, 4 * m, ffq), F32),
                pltpu.VMEM((ys, 4 * m, ff), BF16),
                pltpu.VMEM((ys, m, 16, kc), BF16),
                pltpu.VMEM((ys, m, 16, kc), BF16),
                pltpu.VMEM((2, 2 * m * ys, width), BF16),
                pltpu.VMEM((16 * m, 16 * m), BF16),
                pltpu.VMEM((16 * m, 16 * m), BF16),
                pltpu.VMEM((4 * m, 4 * m), BF16),
                pltpu.VMEM((4 * m, 4 * m), BF16),
                dma,
            ]
            + [dma((ys,))] * 10,
            compiler_params=pltpu.CompilerParams(
                collective_id=0, has_side_effects=True, vmem_limit_bytes=48 * 1024 * 1024
            ),
        )(tokens, probe, cotangent, expert_ids, weight[0])

    in_specs = (
        P("expert", "replica"),
        P("expert", "replica"),
        P("expert", None),
        P("expert", None),
        P("expert", "replica", None),
    )
    out_specs = (P("expert", "replica"), P("expert", "replica"))
    return jax.shard_map(shards, mesh=mesh, in_specs=in_specs, out_specs=out_specs, check_vma=False)
```

```python
import functools

import jax
import jax.numpy as jnp
from jax import lax
from jax.experimental import pallas as pl
from jax.experimental.pallas import tpu as pltpu
from jax.sharding import PartitionSpec as P

CHUNKS = 4
AHEAD = 2
LAG_SUM = 1
LAG_BACK = 2
MESH = pl.DeviceIdType.MESH
F32 = jnp.float32
BF16 = jnp.bfloat16
LANES = 128


def mm(a, b):
    return jnp.dot(a, b, preferred_element_type=F32)


def iota(shape, dim):
    return lax.broadcasted_iota(jnp.int32, shape, dim)


def position(zs, ys):
    me = lax.axis_index("expert")
    return me, me // (2 * ys), lax.rem(me // 2, ys), lax.rem(me, 2)


def targets(zs, ys, ids_row, as_row):
    n = ids_row.shape[1]
    _, z, y, core = position(zs, ys)
    row, col = iota((n, n), 0), iota((n, n), 1)
    ids_col = jnp.sum(
        jnp.where(row == col, ids_row.astype(F32), 0.0), axis=1, keepdims=True
    ).astype(jnp.int32)
    same = ids_col == ids_row
    if as_row:
        slot = jnp.sum(jnp.where(same & (row < col), 1.0, 0.0), axis=0, keepdims=True)
        ids = ids_row
    else:
        slot = jnp.sum(jnp.where(same & (col < row), 1.0, 0.0), axis=1, keepdims=True)
        ids = ids_col
    to_core, to_y, to_z = ids % 2, (ids // 2) % ys, ids // (2 * ys)
    dz = (to_z - z + zs) % zs
    diagonal = (to_y - y - dz + (zs + 2) * ys) % ys
    block = (diagonal * zs + dz) * 2 + (to_core + core) % 2
    return 4 * block + slot.astype(jnp.int32)


def exchange(
    zs, ys, reps, chunks,
    x_hbm, p_hbm, cot_hbm, ids_hbm, w_hbm,
    rows_hbm,
    data, ids_ref, w, fsend, frecv, part, rsrecv, act, bsend, brecv, rows,
    in_sem, out_sem, f_ss, f_rs, r_ss, r_rs, a_ss, a_rs, b_ss, b_rs,
):
    experts = 2 * zs * ys
    m = experts // chunks
    n, width = x_hbm.shape
    tiles = width // LANES
    ffq = part.shape[2] // reps
    me, z, y, core = position(zs, ys)
    rep = lax.axis_index("replica")

    def partner(c, i, forward):
        block = c * m + i
        diagonal, dz, rc = block // (2 * zs), lax.rem(block // 2, zs), lax.rem(block, 2)
        if forward:
            zz, yy = lax.rem(z + dz, zs), lax.rem(y + dz + diagonal, ys)
        else:
            zz, yy = lax.rem(z + zs - dz, zs), lax.rem(y + (zs + 2) * ys - dz - diagonal, ys)
        return (zz * ys + yy) * 2 + lax.rem(core + rc, 2)

    def quarter(r):
        return pl.ds(pl.multiple_of(r * ffq, ffq), ffq)

    loads = [
        pltpu.make_async_copy(a, b, in_sem.at[i])
        for i, (a, b) in enumerate([
            (ids_hbm, ids_ref),
            (x_hbm, data.at[pl.ds(0, n), pl.ds(0, width)]),
            (p_hbm, data.at[pl.ds(n, n), pl.ds(0, width)]),
            (
                cot_hbm.at[:, pl.ds(pl.multiple_of(rep * ffq, LANES), LANES)],
                data.at[pl.ds(0, n), pl.ds(width, LANES)],
            ),
            (
                cot_hbm.at[:, pl.ds(pl.multiple_of(rep * ffq + LANES, LANES), LANES)],
                data.at[pl.ds(n, n), pl.ds(width, LANES)],
            ),
            (w_hbm, w),
        ])
    ]
    for load in loads:
        load.start()

    barrier = pltpu.get_barrier_semaphore()

    def greet(i, carry):
        pl.semaphore_signal(
            barrier, inc=1, device_id=(lax.rem(me + i, experts), rep), device_id_type=MESH
        )
        return carry

    for j in range(1, reps):
        pl.semaphore_signal(
            barrier, inc=1, device_id=(me, lax.rem(rep + j, reps)), device_id_type=MESH
        )
    lax.fori_loop(1, experts, greet, 0)

    loads[0].wait()
    tgt = targets(zs, ys, ids_ref[...], True)
    tgt = jnp.concatenate([tgt, tgt + 2], axis=1)
    for load in loads[1:5]:
        load.wait()

    def whole(ref, c, sem, own):
        if not own:
            pltpu.make_async_copy(ref.at[c], ref.at[c], sem.at[c]).wait()
            return

        @pl.when(c == 0)
        def _():
            some = ref.at[0, pl.ds(1, m - 1)]
            pltpu.make_async_copy(some, some, sem.at[0]).wait()

        @pl.when(c > 0)
        def _():
            pltpu.make_async_copy(ref.at[c], ref.at[c], sem.at[c]).wait()

    def others(ref, c, sem):
        some = ref.at[c, :, pl.ds(0, (reps - 1) * ffq)]
        pltpu.make_async_copy(some, some, sem.at[c]).wait()

    def spread(ref, c, value):
        for t in range(value.shape[1] // LANES):
            ref[c, :, t] = value[:, t * LANES:(t + 1) * LANES].reshape(m, 4, LANES)

    def gather(ref, c, count):
        return jnp.concatenate([ref[c, :, t].reshape(4 * m, LANES) for t in range(count)], axis=1)

    def exchange_blocks(src, dst, c, forward, ss, rs):
        @pl.when(c == 0)
        def _():
            dst[0, 0] = src[0, 0]

        def one(i, carry):
            pltpu.make_async_remote_copy(
                src_ref=src.at[c, i], dst_ref=dst.at[c, i],
                send_sem=ss.at[c], recv_sem=rs.at[c],
                device_id=(partner(c, i, forward), rep), device_id_type=MESH,
            ).start()
            return carry

        lax.fori_loop(jnp.where(c == 0, 1, 0), m, one, 0)

    def pack(c):
        route = jnp.where(iota((4 * m, 2 * n), 0) + c * (4 * m) == tgt, 1.0, 0.0).astype(BF16)
        spread(fsend, c, mm(route, data[...]).astype(BF16))

    def send(c):
        exchange_blocks(fsend, frecv, c, True, f_ss, f_rs)

    def project(c):
        whole(frecv, c, f_rs, True)
        part[c] = mm(gather(frecv, c, tiles), w[...])
        for j in range(1, reps):
            to = lax.rem(rep + j, reps)
            pltpu.make_async_remote_copy(
                src_ref=part.at[c, :, quarter(to)], dst_ref=rsrecv.at[c, j - 1],
                send_sem=r_ss.at[c], recv_sem=r_rs.at[c],
                device_id=(me, to), device_id_type=MESH,
            ).start()

    def activate(c):
        whole(rsrecv, c, r_rs, False)
        total = part[c, :, quarter(rep)]
        for j in range(reps - 1):
            total = total + rsrecv[c, j]
        early = iota((4 * m, 1), 0) % 4 < 2
        cot = frecv[c, :, tiles].reshape(4 * m, LANES).astype(F32)
        cot = jnp.concatenate(
            [
                jnp.where(early, cot, pltpu.roll(cot, 2, 0)),
                jnp.where(early, pltpu.roll(cot, 4 * m - 2, 0), cot),
            ],
            axis=1,
        )
        pre = jnp.where(early, total, pltpu.roll(total, 2, 0))
        sig = 1.0 / (1.0 + jnp.exp(-pre))
        first = sig * (1.0 + pre * (1.0 - sig))
        second = sig * (1.0 - sig) * (2.0 + pre * (1.0 - 2.0 * sig)) * total
        act[c, :, quarter(rep)] = (cot * jnp.where(early, first, second)).astype(BF16)
        for j in range(1, reps):
            to = lax.rem(rep + j, reps)
            pltpu.make_async_remote_copy(
                src_ref=act.at[c, :, quarter(rep)], dst_ref=act.at[c, :, quarter(rep)],
                send_sem=a_ss.at[c], recv_sem=a_rs.at[c],
                device_id=(me, to), device_id_type=MESH,
            ).start()

    def give_back(c):
        others(act, c, a_rs)
        back = lax.dot_general(
            act[c], w[...], (((1,), (1,)), ((), ())), preferred_element_type=F32
        )
        spread(bsend, c, back.astype(BF16))
        exchange_blocks(bsend, brecv, c, False, b_ss, b_rs)

    pack(0)
    pl.semaphore_wait(barrier, experts - 1 + reps - 1)
    send(0)

    def dispatch(c, carry):
        pack(c)
        send(c)
        return carry

    ahead = min(AHEAD, chunks)
    lax.fori_loop(1, ahead, dispatch, 0)
    loads[5].wait()

    def step(s, carry):
        @pl.when(s + ahead < chunks)
        def _():
            dispatch(s + ahead, 0)

        @pl.when(s < chunks)
        def _():
            project(s)

        @pl.when((s >= LAG_SUM) & (s < chunks + LAG_SUM))
        def _():
            activate(s - LAG_SUM)

        @pl.when(s >= LAG_BACK)
        def _():
            give_back(s - LAG_BACK)

        return carry

    lax.fori_loop(0, chunks + LAG_BACK, step, 0)

    def collect(c, carry):
        whole(brecv, c, b_rs, True)
        rows[c] = gather(brecv, c, tiles)
        pltpu.make_async_copy(rows.at[c], rows_hbm.at[c], out_sem).start()
        return carry

    lax.fori_loop(0, chunks, collect, 0)
    pltpu.make_async_copy(rows, rows_hbm, out_sem).wait()

    def drain(c, carry):
        whole(fsend, c, f_ss, True)
        whole(bsend, c, b_ss, True)
        others(part, c, r_ss)
        others(act, c, a_ss)
        return carry

    lax.fori_loop(0, chunks, drain, 0)


def combine(zs, ys, ids_ref, rows_ref, grad_ref, hv_ref):
    tgt = targets(zs, ys, ids_ref[...], False)
    n, count = tgt.shape[0], rows_ref.shape[0]
    tgt = jnp.concatenate([tgt, tgt + 2], axis=0)
    pick = jnp.where(iota((2 * n, count), 1) == tgt, 1.0, 0.0).astype(BF16)
    got = mm(pick, rows_ref[...]).astype(BF16)
    grad_ref[...] = got[:n]
    hv_ref[...] = got[n:]


def solution(mesh):
    experts, reps = mesh.shape["expert"], mesh.shape["replica"]
    zs = {128: 8, 8: 2}[experts]
    ys = experts // (2 * zs)
    chunks = min(CHUNKS, ys)
    m = experts // chunks

    def shards(tokens, probe, cotangent, expert_ids, weight):
        n, width = tokens.shape
        ff = weight.shape[2]
        ffq = ff // reps
        tiles = width // LANES
        anywhere = pl.BlockSpec(memory_space=pl.ANY)
        vmem = pl.BlockSpec(memory_space=pltpu.VMEM)
        dma = pltpu.SemaphoreType.DMA
        ids = expert_ids.reshape(1, n)
        rows = pl.pallas_call(
            functools.partial(exchange, zs, ys, reps, chunks),
            out_shape=jax.ShapeDtypeStruct((chunks, 4 * m, width), BF16),
            in_specs=[anywhere] * 5,
            out_specs=anywhere,
            scratch_shapes=[
                pltpu.VMEM((2 * n, width + LANES), BF16),
                pltpu.VMEM((1, n), jnp.int32),
                pltpu.VMEM((width, ff), BF16),
                pltpu.VMEM((chunks, m, tiles + 1, 4, LANES), BF16),
                pltpu.VMEM((chunks, m, tiles + 1, 4, LANES), BF16),
                pltpu.VMEM((chunks, 4 * m, ff), F32),
                pltpu.VMEM((chunks, reps - 1, 4 * m, ffq), F32),
                pltpu.VMEM((chunks, 4 * m, ff), BF16),
                pltpu.VMEM((chunks, m, tiles, 4, LANES), BF16),
                pltpu.VMEM((chunks, m, tiles, 4, LANES), BF16),
                pltpu.VMEM((chunks, 4 * m, width), BF16),
                dma((6,)),
                dma,
            ]
            + [dma((chunks,))] * 8,
            compiler_params=pltpu.CompilerParams(
                collective_id=0, has_side_effects=True, vmem_limit_bytes=60 * 1024 * 1024
            ),
        )(tokens, probe, cotangent, ids, weight[0])
        return pl.pallas_call(
            functools.partial(combine, zs, ys),
            out_shape=[jax.ShapeDtypeStruct((n, width), BF16)] * 2,
            in_specs=[vmem] * 2,
            out_specs=[vmem] * 2,
            compiler_params=pltpu.CompilerParams(vmem_limit_bytes=60 * 1024 * 1024),
        )(ids, rows.reshape(4 * experts, width))

    in_specs = (
        P("expert", "replica"),
        P("expert", "replica"),
        P("expert", None),
        P("expert", None),
        P("expert", "replica", None),
    )
    out_specs = (P("expert", "replica"), P("expert", "replica"))
    return jax.shard_map(shards, mesh=mesh, in_specs=in_specs, out_specs=out_specs, check_vma=False)
```

```python
import functools

import jax
import jax.numpy as jnp
from jax import lax
from jax.experimental import pallas as pl
from jax.experimental.pallas import tpu as pltpu
from jax.sharding import PartitionSpec as P

SIZES = (32, 32, 32, 32)
SCHEDULE = ""
AHEAD = 2
LAG_SUM = 1
LAG_BACK = 2
LAG_COLLECT = 4
MESH = pl.DeviceIdType.MESH
F32 = jnp.float32
BF16 = jnp.bfloat16
LANES = 128


def mm(a, b):
    return jnp.dot(a, b, preferred_element_type=F32)


def iota(shape, dim):
    return lax.broadcasted_iota(jnp.int32, shape, dim)


def position(zs, ys):
    me = lax.axis_index("expert")
    return me, me // (2 * ys), lax.rem(me // 2, ys), lax.rem(me, 2)


def targets(zs, ys, ids_row, as_row):
    n = ids_row.shape[1]
    _, z, y, core = position(zs, ys)
    row, col = iota((n, n), 0), iota((n, n), 1)
    ids_col = jnp.sum(
        jnp.where(row == col, ids_row.astype(F32), 0.0), axis=1, keepdims=True
    ).astype(jnp.int32)
    same = ids_col == ids_row
    if as_row:
        slot = jnp.sum(jnp.where(same & (row < col), 1.0, 0.0), axis=0, keepdims=True)
        ids = ids_row
    else:
        slot = jnp.sum(jnp.where(same & (col < row), 1.0, 0.0), axis=1, keepdims=True)
        ids = ids_col
    to_core, to_y, to_z = ids % 2, (ids // 2) % ys, ids // (2 * ys)
    dz = (to_z - z + zs) % zs
    diagonal = (to_y - y - dz + (zs + 2) * ys) % ys
    block = (diagonal * zs + dz) * 2 + (to_core + core) % 2
    return 4 * block + slot.astype(jnp.int32)


def plan(count):
    if count == len(SIZES) and SCHEDULE:
        return [(step[0], int(step[1:])) for step in SCHEDULE.split()]
    order = []
    for s in range(count + LAG_COLLECT):
        for name, lag in (
            ("D", -AHEAD), ("P", 0), ("A", LAG_SUM), ("B", LAG_BACK), ("C", LAG_COLLECT)
        ):
            first = range(min(AHEAD, count)) if s == 0 and name == "D" else ()
            order += [(name, c) for c in first]
            if 0 <= s - lag < count:
                order.append((name, s - lag))
    return order


def exchange(
    zs, ys, reps, sizes,
    x_hbm, p_hbm, cot_hbm, ids_hbm, w_hbm,
    grad_ref, hv_ref,
    data, ids_ref, w, fsend, frecv, part, rsrecv, act, bsend, brecv, total,
    in_sem, f_ss, f_rs, r_ss, r_rs, a_ss, a_rs, b_ss, b_rs,
):
    experts = 2 * zs * ys
    starts = [sum(sizes[:c]) for c in range(len(sizes))]
    n, width = x_hbm.shape
    tiles = width // LANES
    ffq = part.shape[1] // reps
    me, z, y, core = position(zs, ys)
    rep = lax.axis_index("replica")

    def partner(block, forward):
        diagonal, dz, rc = block // (2 * zs), lax.rem(block // 2, zs), lax.rem(block, 2)
        if forward:
            zz, yy = lax.rem(z + dz, zs), lax.rem(y + dz + diagonal, ys)
        else:
            zz, yy = lax.rem(z + zs - dz, zs), lax.rem(y + (zs + 2) * ys - dz - diagonal, ys)
        return (zz * ys + yy) * 2 + lax.rem(core + rc, 2)

    def quarter(r):
        return pl.ds(pl.multiple_of(r * ffq, ffq), ffq)

    def blocks_of(c):
        return pl.ds(starts[c], sizes[c])

    def sent_of(c):
        skip = 1 if c == 0 else 0
        return pl.ds(starts[c] + skip, sizes[c] - skip)

    def rows_of(c):
        return pl.ds(4 * starts[c], 4 * sizes[c])

    loads = [
        pltpu.make_async_copy(a, b, in_sem.at[i])
        for i, (a, b) in enumerate([
            (ids_hbm, ids_ref),
            (x_hbm, data.at[pl.ds(0, n), pl.ds(0, width)]),
            (p_hbm, data.at[pl.ds(n, n), pl.ds(0, width)]),
            (
                cot_hbm.at[:, pl.ds(pl.multiple_of(rep * ffq, LANES), LANES)],
                data.at[pl.ds(0, n), pl.ds(width, LANES)],
            ),
            (
                cot_hbm.at[:, pl.ds(pl.multiple_of(rep * ffq + LANES, LANES), LANES)],
                data.at[pl.ds(n, n), pl.ds(width, LANES)],
            ),
            (w_hbm, w),
        ])
    ]
    for load in loads[:5]:
        load.start()

    barrier = pltpu.get_barrier_semaphore()

    def greet(i, carry):
        pl.semaphore_signal(
            barrier, inc=1, device_id=(lax.rem(me + i, experts), rep), device_id_type=MESH
        )
        return carry

    for j in range(1, reps):
        pl.semaphore_signal(
            barrier, inc=1, device_id=(me, lax.rem(rep + j, reps)), device_id_type=MESH
        )
    lax.fori_loop(1, experts, greet, 0)

    loads[0].wait()
    tgt = targets(zs, ys, ids_ref[...], True)
    tgt = jnp.concatenate([tgt, tgt + 2], axis=1)
    tgt_col = targets(zs, ys, ids_ref[...], False)
    tgt_col = jnp.concatenate([tgt_col, tgt_col + 2], axis=0)
    for load in loads[1:5]:
        load.wait()
    loads[5].start()

    def wait(piece, sem):
        pltpu.make_async_copy(piece, piece, sem).wait()

    def others(ref, c):
        return ref.at[rows_of(c), pl.ds(0, (reps - 1) * ffq)]

    def spread(ref, c, value):
        for t in range(value.shape[1] // LANES):
            tile = value[:, t * LANES:(t + 1) * LANES]
            ref[blocks_of(c), t] = tile.reshape(sizes[c], 4, LANES)

    def gather(ref, c, count):
        return jnp.concatenate(
            [ref[blocks_of(c), t].reshape(4 * sizes[c], LANES) for t in range(count)], axis=1
        )

    def exchange_blocks(src, dst, c, forward, ss, rs):
        if c == 0:
            dst[0] = src[0]

        def one(block, carry):
            pltpu.make_async_remote_copy(
                src_ref=src.at[block], dst_ref=dst.at[block],
                send_sem=ss.at[c], recv_sem=rs.at[c],
                device_id=(partner(block, forward), rep), device_id_type=MESH,
            ).start()
            return carry

        lax.fori_loop(starts[c] + (1 if c == 0 else 0), starts[c] + sizes[c], one, 0)

    def to_replicas(src, dst, c, ss, rs):
        for j in range(1, reps):
            to = lax.rem(rep + j, reps)
            pltpu.make_async_remote_copy(
                src_ref=src(to), dst_ref=dst(j), send_sem=ss.at[c], recv_sem=rs.at[c],
                device_id=(me, to), device_id_type=MESH,
            ).start()

    def pack(c):
        at = iota((4 * sizes[c], 2 * n), 0) + 4 * starts[c]
        route = jnp.where(at == tgt, 1.0, 0.0).astype(BF16)
        spread(fsend, c, mm(route, data[...]).astype(BF16))

    def dispatch(c):
        pack(c)
        if c == 0:
            pl.semaphore_wait(barrier, experts - 1 + reps - 1)
        exchange_blocks(fsend, frecv, c, True, f_ss, f_rs)

    def project(c):
        if c == 0:
            loads[5].wait()
        wait(frecv.at[sent_of(c)], f_rs.at[c])
        part[rows_of(c)] = mm(gather(frecv, c, tiles), w[...])
        to_replicas(
            lambda to: part.at[rows_of(c), quarter(to)],
            lambda j: rsrecv.at[j - 1, rows_of(c)],
            c, r_ss, r_rs,
        )

    def activate(c):
        wait(rsrecv.at[:, rows_of(c)], r_rs.at[c])
        count = 4 * sizes[c]
        summed = part[rows_of(c), quarter(rep)]
        for j in range(reps - 1):
            summed = summed + rsrecv[j, rows_of(c)]
        early = iota((count, 1), 0) % 4 < 2
        cot = frecv[blocks_of(c), tiles].reshape(count, LANES).astype(F32)
        cot = jnp.concatenate(
            [
                jnp.where(early, cot, pltpu.roll(cot, 2, 0)),
                jnp.where(early, pltpu.roll(cot, count - 2, 0), cot),
            ],
            axis=1,
        )
        pre = jnp.where(early, summed, pltpu.roll(summed, 2, 0))
        sig = 1.0 / (1.0 + jnp.exp(-pre))
        first = sig * (1.0 + pre * (1.0 - sig))
        second = sig * (1.0 - sig) * (2.0 + pre * (1.0 - 2.0 * sig)) * summed
        act[rows_of(c), quarter(rep)] = (cot * jnp.where(early, first, second)).astype(BF16)
        mine = act.at[rows_of(c), quarter(rep)]
        to_replicas(lambda to: mine, lambda j: mine, c, a_ss, a_rs)

    def give_back(c):
        wait(others(act, c), a_rs.at[c])
        back = lax.dot_general(
            act[rows_of(c)], w[...], (((1,), (1,)), ((), ())), preferred_element_type=F32
        )
        spread(bsend, c, back.astype(BF16))
        exchange_blocks(bsend, brecv, c, False, b_ss, b_rs)

    def collect(c):
        wait(brecv.at[sent_of(c)], b_rs.at[c])
        at = iota((2 * n, 4 * sizes[c]), 1) + 4 * starts[c]
        pick = jnp.where(at == tgt_col, 1.0, 0.0).astype(BF16)
        got = mm(pick, gather(brecv, c, tiles))
        if c > 0:
            got = got + total[...]
        if c < len(sizes) - 1:
            total[...] = got
        else:
            grad_ref[...] = got[:n].astype(BF16)
            hv_ref[...] = got[n:].astype(BF16)

    steps = dict(D=dispatch, P=project, A=activate, B=give_back, C=collect)
    for name, c in plan(len(sizes)):
        steps[name](c)

    for c in range(len(sizes)):
        wait(fsend.at[sent_of(c)], f_ss.at[c])
        wait(bsend.at[sent_of(c)], b_ss.at[c])
        wait(others(part, c), r_ss.at[c])
        wait(others(act, c), a_ss.at[c])


def solution(mesh):
    experts, reps = mesh.shape["expert"], mesh.shape["replica"]
    zs = {128: 8, 8: 2}[experts]
    ys = experts // (2 * zs)
    sizes = SIZES if sum(SIZES) == experts else (2, 4, 2)
    count = len(sizes)

    def shards(tokens, probe, cotangent, expert_ids, weight):
        n, width = tokens.shape
        ff = weight.shape[2]
        ffq = ff // reps
        tiles = width // LANES
        outside = pl.BlockSpec(memory_space=pltpu.HBM)
        dma = pltpu.SemaphoreType.DMA
        return pl.pallas_call(
            functools.partial(exchange, zs, ys, reps, sizes),
            out_shape=[jax.ShapeDtypeStruct((n, width), BF16)] * 2,
            in_specs=[outside] * 5,
            out_specs=[pl.BlockSpec(memory_space=pltpu.VMEM)] * 2,
            scratch_shapes=[
                pltpu.VMEM((2 * n, width + LANES), BF16),
                pltpu.VMEM((1, n), jnp.int32),
                pltpu.VMEM((width, ff), BF16),
                pltpu.VMEM((experts, tiles + 1, 4, LANES), BF16),
                pltpu.VMEM((experts, tiles + 1, 4, LANES), BF16),
                pltpu.VMEM((4 * experts, ff), F32),
                pltpu.VMEM((reps - 1, 4 * experts, ffq), F32),
                pltpu.VMEM((4 * experts, ff), BF16),
                pltpu.VMEM((experts, tiles, 4, LANES), BF16),
                pltpu.VMEM((experts, tiles, 4, LANES), BF16),
                pltpu.VMEM((2 * n, width), F32),
                dma((6,)),
            ]
            + [dma((count,))] * 8,
            compiler_params=pltpu.CompilerParams(
                collective_id=0, has_side_effects=True, vmem_limit_bytes=44 * 1024 * 1024
            ),
        )(*[pltpu.with_memory_space_constraint(a, pltpu.HBM) for a in (tokens, probe, cotangent, expert_ids.reshape(1, n), weight[0])])

    in_specs = (
        P("expert", "replica"),
        P("expert", "replica"),
        P("expert", None),
        P("expert", None),
        P("expert", "replica", None),
    )
    out_specs = (P("expert", "replica"), P("expert", "replica"))
    return jax.shard_map(shards, mesh=mesh, in_specs=in_specs, out_specs=out_specs, check_vma=False)
```

```python
import functools

import jax
import jax.numpy as jnp
from jax import lax
from jax.experimental import pallas as pl
from jax.experimental.pallas import tpu as pltpu
from jax.sharding import PartitionSpec as P

SIZES = (16, 16, 16, 16, 16, 16, 16, 16)
SCHEDULE = ""
AHEAD = 3
LAG_SUM = 2
LAG_BACK = 4
LAG_COLLECT = 12
MESH = pl.DeviceIdType.MESH
F32 = jnp.float32
BF16 = jnp.bfloat16
LANES = 128


def mm(a, b):
    return jnp.dot(a, b, preferred_element_type=F32)


def iota(shape, dim):
    return lax.broadcasted_iota(jnp.int32, shape, dim)


def position(zs, ys):
    me = lax.axis_index("expert")
    return me, me // (2 * ys), lax.rem(me // 2, ys), lax.rem(me, 2)


def targets(zs, ys, ids_row, as_row):
    n = ids_row.shape[1]
    _, z, y, core = position(zs, ys)
    row, col = iota((n, n), 0), iota((n, n), 1)
    ids_col = jnp.sum(
        jnp.where(row == col, ids_row.astype(F32), 0.0), axis=1, keepdims=True
    ).astype(jnp.int32)
    same = ids_col == ids_row
    if as_row:
        slot = jnp.sum(jnp.where(same & (row < col), 1.0, 0.0), axis=0, keepdims=True)
        ids = ids_row
    else:
        slot = jnp.sum(jnp.where(same & (col < row), 1.0, 0.0), axis=1, keepdims=True)
        ids = ids_col
    to_core, to_y, to_z = ids % 2, (ids // 2) % ys, ids // (2 * ys)
    dz = (to_z - z + zs) % zs
    diagonal = (to_y - y - dz + (zs + 2) * ys) % ys
    block = (diagonal * zs + dz) * 2 + (to_core + core) % 2
    return 4 * block + slot.astype(jnp.int32)


def plan(count):
    if count == len(SIZES) and SCHEDULE:
        return [(step[0], int(step[1:])) for step in SCHEDULE.split()]
    order = []
    for s in range(count + LAG_COLLECT):
        for name, lag in (
            ("D", -AHEAD), ("P", 0), ("A", LAG_SUM), ("B", LAG_BACK), ("C", LAG_COLLECT)
        ):
            first = range(min(AHEAD, count)) if s == 0 and name == "D" else ()
            order += [(name, c) for c in first]
            if 0 <= s - lag < count:
                order.append((name, s - lag))
    return order


def exchange(
    zs, ys, reps, sizes,
    x_hbm, p_hbm, cot_hbm, ids_hbm, w_hbm,
    grad_ref, hv_ref,
    data, ids_ref, w, fsend, frecv, part, rsrecv, act, bsend, brecv, total, back_targets,
    in_sem, f_ss, f_rs, r_ss, r_rs, a_ss, a_rs, b_ss, b_rs,
):
    experts = 2 * zs * ys
    starts = [sum(sizes[:c]) for c in range(len(sizes))]
    n, width = x_hbm.shape
    tiles = width // LANES
    ffq = part.shape[1] // reps
    me, z, y, core = position(zs, ys)
    rep = lax.axis_index("replica")

    def partner(block, forward):
        diagonal, dz, rc = block // (2 * zs), lax.rem(block // 2, zs), lax.rem(block, 2)
        if forward:
            zz, yy = lax.rem(z + dz, zs), lax.rem(y + dz + diagonal, ys)
        else:
            zz, yy = lax.rem(z + zs - dz, zs), lax.rem(y + (zs + 2) * ys - dz - diagonal, ys)
        return (zz * ys + yy) * 2 + lax.rem(core + rc, 2)

    def quarter(r):
        return pl.ds(pl.multiple_of(r * ffq, ffq), ffq)

    def blocks_of(c):
        return pl.ds(starts[c], sizes[c])

    def sent_of(c):
        skip = 1 if c == 0 else 0
        return pl.ds(starts[c] + skip, sizes[c] - skip)

    def rows_of(c):
        return pl.ds(4 * starts[c], 4 * sizes[c])

    loads = [
        pltpu.make_async_copy(a, b, in_sem.at[i])
        for i, (a, b) in enumerate([
            (ids_hbm, ids_ref),
            (x_hbm, data.at[pl.ds(0, n), pl.ds(0, width)]),
            (p_hbm, data.at[pl.ds(n, n), pl.ds(0, width)]),
            (
                cot_hbm.at[:, pl.ds(pl.multiple_of(rep * ffq, LANES), LANES)],
                data.at[pl.ds(0, n), pl.ds(width, LANES)],
            ),
            (
                cot_hbm.at[:, pl.ds(pl.multiple_of(rep * ffq + LANES, LANES), LANES)],
                data.at[pl.ds(n, n), pl.ds(width, LANES)],
            ),
            (w_hbm, w),
        ])
    ]
    for load in loads[:5]:
        load.start()

    barrier = pltpu.get_barrier_semaphore()

    def greet(i, carry):
        pl.semaphore_signal(
            barrier, inc=1, device_id=(lax.rem(me + i, experts), rep), device_id_type=MESH
        )
        return carry

    for j in range(1, reps):
        pl.semaphore_signal(
            barrier, inc=1, device_id=(me, lax.rem(rep + j, reps)), device_id_type=MESH
        )
    lax.fori_loop(1, experts, greet, 0)

    loads[0].wait()
    tgt = targets(zs, ys, ids_ref[...], True)
    tgt = jnp.concatenate([tgt, tgt + 2], axis=1)
    for load in loads[1:5]:
        load.wait()
    loads[5].start()

    def wait(piece, sem):
        pltpu.make_async_copy(piece, piece, sem).wait()

    def others(ref, c):
        return ref.at[rows_of(c), pl.ds(0, (reps - 1) * ffq)]

    def spread(ref, c, value):
        for t in range(value.shape[1] // LANES):
            tile = value[:, t * LANES:(t + 1) * LANES]
            ref[blocks_of(c), t] = tile.reshape(sizes[c], 4, LANES)

    def gather(ref, c, count):
        return jnp.concatenate(
            [ref[blocks_of(c), t].reshape(4 * sizes[c], LANES) for t in range(count)], axis=1
        )

    def exchange_blocks(src, dst, c, forward, ss, rs):
        if c == 0:
            dst[0] = src[0]

        def one(block, carry):
            pltpu.make_async_remote_copy(
                src_ref=src.at[block], dst_ref=dst.at[block],
                send_sem=ss.at[c], recv_sem=rs.at[c],
                device_id=(partner(block, forward), rep), device_id_type=MESH,
            ).start()
            return carry

        lax.fori_loop(starts[c] + (1 if c == 0 else 0), starts[c] + sizes[c], one, 0)

    def to_replicas(src, dst, c, ss, rs):
        for j in range(1, reps):
            to = lax.rem(rep + j, reps)
            pltpu.make_async_remote_copy(
                src_ref=src(to), dst_ref=dst(j), send_sem=ss.at[c], recv_sem=rs.at[c],
                device_id=(me, to), device_id_type=MESH,
            ).start()

    def pack(c):
        at = iota((4 * sizes[c], 2 * n), 0) + 4 * starts[c]
        route = jnp.where(at == tgt, 1.0, 0.0).astype(BF16)
        spread(fsend, c, mm(route, data[...]).astype(BF16))

    def dispatch(c):
        pack(c)
        if c == 0:
            pl.semaphore_wait(barrier, experts - 1 + reps - 1)
        exchange_blocks(fsend, frecv, c, True, f_ss, f_rs)
        if c == len(sizes) - 1:
            tgt_col = targets(zs, ys, ids_ref[...], False)
            back_targets[...] = jnp.concatenate([tgt_col, tgt_col + 2], axis=0)

    def project(c):
        if c == 0:
            loads[5].wait()
        wait(frecv.at[sent_of(c)], f_rs.at[c])
        part[rows_of(c)] = mm(gather(frecv, c, tiles), w[...])
        to_replicas(
            lambda to: part.at[rows_of(c), quarter(to)],
            lambda j: rsrecv.at[j - 1, rows_of(c)],
            c, r_ss, r_rs,
        )

    def activate(c):
        wait(rsrecv.at[:, rows_of(c)], r_rs.at[c])
        count = 4 * sizes[c]
        summed = part[rows_of(c), quarter(rep)]
        for j in range(reps - 1):
            summed = summed + rsrecv[j, rows_of(c)]
        early = iota((count, 1), 0) % 4 < 2
        cot = frecv[blocks_of(c), tiles].reshape(count, LANES).astype(F32)
        cot = jnp.concatenate(
            [
                jnp.where(early, cot, pltpu.roll(cot, 2, 0)),
                jnp.where(early, pltpu.roll(cot, count - 2, 0), cot),
            ],
            axis=1,
        )
        pre = jnp.where(early, summed, pltpu.roll(summed, 2, 0))
        sig = 1.0 / (1.0 + jnp.exp(-pre))
        first = sig * (1.0 + pre * (1.0 - sig))
        second = sig * (1.0 - sig) * (2.0 + pre * (1.0 - 2.0 * sig)) * summed
        act[rows_of(c), quarter(rep)] = (cot * jnp.where(early, first, second)).astype(BF16)
        mine = act.at[rows_of(c), quarter(rep)]
        to_replicas(lambda to: mine, lambda j: mine, c, a_ss, a_rs)

    def give_back(c):
        wait(others(act, c), a_rs.at[c])
        back = lax.dot_general(
            act[rows_of(c)], w[...], (((1,), (1,)), ((), ())), preferred_element_type=F32
        )
        spread(bsend, c, back.astype(BF16))
        exchange_blocks(bsend, brecv, c, False, b_ss, b_rs)

    def collect(c):
        tgt_col = back_targets[...]
        wait(brecv.at[sent_of(c)], b_rs.at[c])
        at = iota((2 * n, 4 * sizes[c]), 1) + 4 * starts[c]
        pick = jnp.where(at == tgt_col, 1.0, 0.0).astype(BF16)
        got = mm(pick, gather(brecv, c, tiles))
        if c > 0:
            got = got + total[...]
        if c < len(sizes) - 1:
            total[...] = got
        else:
            grad_ref[...] = got[:n].astype(BF16)
            hv_ref[...] = got[n:].astype(BF16)

    steps = dict(D=dispatch, P=project, A=activate, B=give_back, C=collect)
    for name, c in plan(len(sizes)):
        steps[name](c)

    for c in range(len(sizes)):
        wait(fsend.at[sent_of(c)], f_ss.at[c])
        wait(bsend.at[sent_of(c)], b_ss.at[c])
        wait(others(part, c), r_ss.at[c])
        wait(others(act, c), a_ss.at[c])


def solution(mesh):
    experts, reps = mesh.shape["expert"], mesh.shape["replica"]
    zs = {128: 8, 8: 2}[experts]
    ys = experts // (2 * zs)
    sizes = SIZES if sum(SIZES) == experts else (2, 4, 2)
    count = len(sizes)

    def shards(tokens, probe, cotangent, expert_ids, weight):
        n, width = tokens.shape
        ff = weight.shape[2]
        ffq = ff // reps
        tiles = width // LANES
        outside = pl.BlockSpec(memory_space=pltpu.HBM)
        dma = pltpu.SemaphoreType.DMA
        return pl.pallas_call(
            functools.partial(exchange, zs, ys, reps, sizes),
            out_shape=[jax.ShapeDtypeStruct((n, width), BF16)] * 2,
            in_specs=[outside] * 5,
            out_specs=[pl.BlockSpec(memory_space=pltpu.VMEM)] * 2,
            scratch_shapes=[
                pltpu.VMEM((2 * n, width + LANES), BF16),
                pltpu.VMEM((1, n), jnp.int32),
                pltpu.VMEM((width, ff), BF16),
                pltpu.VMEM((experts, tiles + 1, 4, LANES), BF16),
                pltpu.VMEM((experts, tiles + 1, 4, LANES), BF16),
                pltpu.VMEM((4 * experts, ff), F32),
                pltpu.VMEM((reps - 1, 4 * experts, ffq), F32),
                pltpu.VMEM((4 * experts, ff), BF16),
                pltpu.VMEM((experts, tiles, 4, LANES), BF16),
                pltpu.VMEM((experts, tiles, 4, LANES), BF16),
                pltpu.VMEM((2 * n, width), F32),
                pltpu.VMEM((2 * n, 1), jnp.int32),
                dma((6,)),
            ]
            + [dma((count,))] * 8,
            compiler_params=pltpu.CompilerParams(
                collective_id=0, has_side_effects=True, vmem_limit_bytes=44 * 1024 * 1024
            ),
        )(*[pltpu.with_memory_space_constraint(a, pltpu.HBM) for a in (tokens, probe, cotangent, expert_ids.reshape(1, n), weight[0])])

    in_specs = (
        P("expert", "replica"),
        P("expert", "replica"),
        P("expert", None),
        P("expert", None),
        P("expert", "replica", None),
    )
    out_specs = (P("expert", "replica"), P("expert", "replica"))
    return jax.shard_map(shards, mesh=mesh, in_specs=in_specs, out_specs=out_specs, check_vma=False)
```
